32 devices in a mesh: section: 2 (over x), dp: 16 (over z, y, core).
Axes of the slice: x: 2, y: 2, z: 4, core: 2. Of those that a mesh axis runs over, the one named last changes fastest.
Arguments:
- center_data: bfloat16 [2, 384, 300], P('section', 'dp'), may hold values from -6 to 6
- edge_data: bfloat16 [2, 384, 100, 300], P('section', 'dp'), may hold values from -6 to 6
- leaf_counts: int32 [384], P('dp'), may hold values from 10 to 100, as said below
- leaf_mask: int32 [384, 100], P('dp'), may hold values 0 or 1
- square_weights: bfloat16 [2, 4, 300, 300], P('section'), may hold values from -0.375 to 0.375
- out_weight: bfloat16 [2, 300, 300], P('section'), may hold values from -1.5 to 1.5
- up_weight: bfloat16 [2, 300, 1200], P('section'), may hold values from -0.375 to 0.375
- down_weight: bfloat16 [2, 1200, 300], P('section'), may hold values from -0.1875 to 0.1875
- norm_gains: bfloat16 [2, 3, 300], P('section'), may hold values from 0.5 to 1.5
- biases: bfloat16 [2, 8, 300], P('section'), may hold values from -1.5 to 1.5
- hidden_bias: bfloat16 [2, 1200], P('section'), may hold values from -1.5 to 1.5
Outputs:
- center_result: bfloat16 [2, 384, 300], P('section', 'dp')
- edge_result: bfloat16 [2, 384, 100, 300], P('section', 'dp')
- grad_square: float32 [2, 4, 300, 300], P('section')
- grad_out_weight: float32 [2, 300, 300], P('section')
- grad_up: float32 [2, 300, 1200], P('section')
- grad_down: float32 [2, 1200, 300], P('section')
- grad_norm_gains: float32 [2, 3, 300], P('section')
- grad_biases: float32 [2, 8, 300], P('section')
- grad_hidden_bias: float32 [2, 1200], P('section')
- norms: float32 [2, 5, 384], P('section', None, 'dp')
The draws below stay inside these ranges and needn't reach their ends.
Inputs may be any that keep to these rules, and one draw needn't show every extreme that they name: The first leaf_counts[g] leaf slots of star g may hold leaves; both ends occur in every draw.
All inputs are finite; a program needn't handle non-finite values. No bound on the sum of `leaf_mask` on one device may be relied on, other than what follows from the above.
Results may differ from the reference program's by a relative error of at most 0.015.
Values may be sent and summed in bfloat16 or wider, within the bound.
A program may use at most 192 MiB of HBM per device.

```python
import jax
import jax.numpy as jnp
from jax import lax

HEADS = 12
D = 300
FF = 1200
SLOTS = 100
MIN_LEAVES = 10
MB_STARS = 4
GRAPHS = 384


def draw_leaf_counts(key, part):
    key = jax.random.fold_in(key, 17)
    count_key, place_key = jax.random.split(key)
    counts = jax.random.randint(count_key, (GRAPHS,), MIN_LEAVES, SLOTS + 1)
    full_star = jax.random.randint(place_key, (), 0, GRAPHS)
    counts = counts.at[full_star].set(SLOTS)
    counts = counts.at[(full_star + GRAPHS // 2) % GRAPHS].set(MIN_LEAVES)
    return counts.astype(jnp.int32)


def set_ends(values, rng, least, high):
    dims = values.shape
    index_at = [jax.random.randint(jax.random.fold_in(rng, axis), (), 0, dims[axis]) for axis in range(len(dims))]
    values = values.at[tuple(index_at)].set(least)
    longest = dims.index(max(dims))
    index_at[longest] = (index_at[longest] + 1) % dims[longest]
    return values.at[tuple(index_at)].set(high)


def levels(key, extent, cuts, smallest, top_value):
    gain = 1.0
    for position, blocks in cuts:
        draws = jax.random.uniform(jax.random.fold_in(jax.random.fold_in(key, 6), position), (blocks,), jnp.float32, smallest / len(cuts), top_value / len(cuts))
        gain = gain * jnp.repeat(jnp.exp(draws), extent[position] // blocks).reshape((-1,) + (1,) * (len(extent) - 1 - position))
    return gain


def gaussian(stream_key, extent, scale, most, cuts=(), held_as=jnp.bfloat16):
    drawn = jax.random.normal(stream_key, extent, jnp.float32) * scale
    if len(cuts) > 0:
        drawn = levels(stream_key, extent, cuts, -0.22, 0.18) * drawn
    return jnp.clip(drawn, min=-most, max=most).astype(held_as)


def setup_inputs(seed: int = 0) -> dict:
    keys = jax.random.split(jax.random.key(seed), 12)
    return {
        "center_data": gaussian(keys[0], (2, GRAPHS, D), 1.0, 6.0, ((0, 2), (1, 16))),
        "edge_data": gaussian(keys[1], (2, GRAPHS, SLOTS, D), 1.0, 6.0, ((0, 2), (1, 16))),
        "leaf_counts": draw_leaf_counts(jax.random.fold_in(keys[11], 71), 0),
        "leaf_mask": set_ends((jax.random.randint(keys[3], (GRAPHS, SLOTS), 0, 5) < 4).astype(jnp.int32), jax.random.fold_in(keys[3], 1), 0, 1),
        "square_weights": gaussian(keys[4], (2, 4, D, D), D ** -0.5, 0.375, ((0, 2),)),
        "out_weight": gaussian(keys[5], (2, D, D), (max(D // 16, 4)) ** -0.5, 1.5, ((0, 2),)),
        "up_weight": gaussian(keys[6], (2, D, FF), D ** -0.5, 0.375, ((0, 2),)),
        "down_weight": gaussian(keys[7], (2, FF, D), FF ** -0.5, 0.1875, ((0, 2),)),
        "norm_gains": jnp.clip(1.0 + 0.1 * jax.random.normal(keys[8], (2, 3, D), jnp.float32), 0.5, 1.5).astype(jnp.bfloat16),
        "biases": gaussian(keys[9], (2, 8, D), 0.3, 1.5, ((0, 2),)),
        "hidden_bias": gaussian(keys[10], (2, FF), 0.3, 1.5, ((0, 2),)),
    }


@jax.custom_vjp
def low(v):
    return lax.optimization_barrier(v.astype(jnp.bfloat16)).astype(jnp.float32)

@jax.custom_vjp
def low_back(v):
    return v

def low_keep(v):
    return (low(v), None)

def low_pass(kept, grad):
    return (grad,)

def back_keep(v):
    return (v, None)

def back_low(kept, grad):
    return (low(grad),)
low.defvjp(low_keep, low_pass)
low_back.defvjp(back_keep, back_low)
EPSILON = 1e-05
PRECISE = lax.Precision.HIGHEST

def layer_norm(values, gain_row, bias_row):
    centred = values - lax.optimization_barrier(jnp.mean(values, axis=-1, keepdims=True))
    spread = lax.optimization_barrier(jnp.mean(centred * centred, axis=-1, keepdims=True))
    return centred * lax.rsqrt(spread + EPSILON) * gain_row + bias_row

def product(operand, factor):
    return jnp.dot(operand, factor, precision=PRECISE, preferred_element_type=jnp.float32)

def rounded_both(values):
    return low(low_back(values))

def root_square(values, axes):
    return jnp.sqrt(lax.optimization_barrier(jnp.mean(values * values, axis=axes)))

def layer(weights, centre, edges, live_slots):
    square, out_matrix, up_matrix, down_matrix, gain_rows, bias_rows, hidden_shift = weights
    star_count, slot_count, model_width = edges.shape
    head_size = model_width // HEADS
    centre_norm = low(layer_norm(centre, gain_rows[0], bias_rows[0]))
    edge_norm = low(layer_norm(edges, gain_rows[1], bias_rows[1]))
    query = rounded_both(product(centre_norm, square[0]) + bias_rows[3])
    key_rows = rounded_both(jnp.concatenate([product(centre_norm, square[1])[:, None], product(edge_norm, square[1])], 1))
    value_rows = rounded_both(jnp.concatenate([product(centre_norm, square[2])[:, None], product(edge_norm, square[2])], 1) + bias_rows[4])
    query_heads = query.reshape(star_count, HEADS, head_size)
    key_heads = key_rows.reshape(star_count, slot_count + 1, HEADS, head_size)
    value_heads = value_rows.reshape(star_count, slot_count + 1, HEADS, head_size)
    raw = jnp.einsum('bhd,blhd->bhl', query_heads, key_heads, precision=PRECISE)
    scores = low_back(raw * head_size ** (-0.5))
    allowed = jnp.concatenate([jnp.ones((star_count, 1), jnp.float32), live_slots], 1)[:, None, :] > 0
    prob_rows = low(jax.nn.softmax(jnp.where(allowed, scores, -1e+30), axis=-1))
    attended = rounded_both(jnp.einsum('bhl,blhd->bhd', prob_rows, value_heads, precision=PRECISE).reshape(star_count, model_width))
    branch_attn = low_back(product(attended, out_matrix) + bias_rows[5])
    middle = centre + branch_attn
    gate_in = rounded_both(edge_norm * centre_norm[:, None, :])
    branch_edge = low_back(product(gate_in, square[3]) + bias_rows[6])
    update = live_slots[:, :, None] * branch_edge
    edges_out = edges + update
    feed_norm = low(layer_norm(middle, gain_rows[2], bias_rows[2]))
    hidden = low_back(product(feed_norm, up_matrix) + hidden_shift)
    active = low(jax.nn.gelu(hidden, approximate=False))
    branch_ffn = low_back(product(active, down_matrix) + bias_rows[7])
    centre_out = middle + branch_ffn
    norm_rows = jnp.stack([root_square(centre_out, -1), root_square(edges_out, (1, 2)), root_square(branch_attn, -1), root_square(update, (1, 2)), root_square(branch_ffn, -1)])
    return (centre_out, edges_out, norm_rows)

def two_layers(weights, centre, edges, live_slots):
    lower_layer = tuple((stacked[0] for stacked in weights))
    upper_layer = tuple((stacked[1] for stacked in weights))
    middle_centre, middle_edges, norms_lower = layer(lower_layer, centre, edges, live_slots)
    final_centre, final_edges, norms_upper = layer(upper_layer, rounded_both(middle_centre), rounded_both(middle_edges), live_slots)
    return ((final_centre, final_edges), jnp.stack([norms_lower, norms_upper]))

def reference(center_data, edge_data, leaf_counts, leaf_mask, square_weights, out_weight, up_weight, down_weight, norm_gains, biases, hidden_bias):
    weights = tuple((stacked.astype(jnp.float32) for stacked in (square_weights, out_weight, up_weight, down_weight, norm_gains, biases, hidden_bias)))
    slot_index = lax.broadcasted_iota(jnp.int32, (GRAPHS, SLOTS), 1)
    live_slots = ((slot_index < leaf_counts[:, None]) & (leaf_mask > 0)).astype(jnp.float32)
    block_count = GRAPHS // MB_STARS
    centre = center_data[0].astype(jnp.float32).reshape(block_count, MB_STARS, D)
    edges = edge_data[0].astype(jnp.float32).reshape(block_count, MB_STARS, SLOTS, D)
    live_blocks = live_slots.reshape(block_count, MB_STARS, SLOTS)
    checked = jax.checkpoint(two_layers)

    def whole(weight_tree, centre_all, edges_all):
        return lax.map(lambda piece: checked(weight_tree, piece[0], piece[1], piece[2]), (centre_all, edges_all, live_blocks))
    outputs, backward, norm_blocks = jax.vjp(whole, weights, centre, edges, has_aux=True)
    cotangent = (center_data[1].astype(jnp.float32).reshape(block_count, MB_STARS, D), edge_data[1].astype(jnp.float32).reshape(block_count, MB_STARS, SLOTS, D))
    grad_weights, grad_centre, grad_edges = backward(cotangent)
    center_result = jnp.stack([grad_centre.reshape(GRAPHS, D), outputs[0].reshape(GRAPHS, D)]).astype(jnp.bfloat16)
    edge_result = jnp.stack([grad_edges.reshape(GRAPHS, SLOTS, D), outputs[1].reshape(GRAPHS, SLOTS, D)]).astype(jnp.bfloat16)
    norms = jnp.transpose(norm_blocks, (1, 2, 0, 3)).reshape(2, 5, GRAPHS)
    return (center_result, edge_result, grad_weights[0], grad_weights[1], grad_weights[2], grad_weights[3], grad_weights[4], grad_weights[5], grad_weights[6], norms)
```

```python
import functools
import math

import jax
import jax.numpy as jnp
from jax import lax
from jax.experimental import pallas as pl
from jax.experimental.pallas import tpu as pltpu
from jax.sharding import PartitionSpec as P

HEADS = 12
HEAD_ROWS = 16
TILE = 8
PAIR = 16
PIECES = 5
LOADS = 4
FIRST_PIECES = 2
MOST_GATHERED = 16
EPSILON = 1e-05
MASKED_SCORE = -1e30
F32 = jnp.float32
BF16 = jnp.bfloat16
MESH_ID = pl.DeviceIdType.MESH


def padded(size):
    return -(-size // 128) * 128


def split_devices(count):
    radices = []
    for _ in range(2):
        if count % 2 == 0 and count > 1:
            radices.append(2)
            count //= 2
    return radices + [count] if count > 1 else radices


def aligned(start):
    return start if isinstance(start, int) else pl.multiple_of(start, PAIR)


def product(operand, factor):
    return lax.dot_general(
        operand, factor, (((1,), (0,)), ((), ())), preferred_element_type=F32
    )


def against(operand, factor):
    return lax.dot_general(
        operand, factor, (((1,), (1,)), ((), ())), preferred_element_type=F32
    )


def outer_sum(operand, factor):
    return lax.dot_general(
        operand, factor, (((0,), (0,)), ((), ())), preferred_element_type=F32
    )


def low(values):
    return values.astype(BF16)


def wide(values):
    return values.astype(F32)


def gelu_parts(values):
    phi = 0.5 * (1.0 + lax.erf(values * (0.5**0.5)))
    density = jnp.exp(-0.5 * values * values) * 0.3989422804014327
    return values * phi, phi + values * density


def sum_pairs(values):
    return values[:TILE] + values[TILE:]


def pad_rows(values):
    return jnp.concatenate([values, jnp.zeros_like(values)], 0)


def flat(values):
    return values.reshape(values.shape[0] * values.shape[1], values.shape[2])


class Sizes:
    def __init__(self, star_count, slot_count, model_width, hidden_width, devices):
        self.stars = star_count
        self.slots = slot_count
        self.width = model_width
        self.hidden = hidden_width
        self.devices = devices
        self.lanes = padded(model_width)
        self.hidden_lanes = padded(hidden_width)
        self.main = self.lanes - 128
        self.groups = star_count // TILE
        self.rows = slot_count * TILE
        self.piece = self.rows // PIECES
        tall = -(-self.piece // 3 // PAIR) * PAIR
        self.short = (self.piece - tall) // 2
        self.tall = tall
        self.over = model_width - self.main
        self.fits = 128 - 2 * self.over
        self.spill = self.over - self.fits
        assert self.short % PAIR == 0 and tall - self.short == PAIR and self.spill > 0
        assert self.short // PAIR * self.spill <= self.fits
        self.within = devices <= MOST_GATHERED
        self.radices = split_devices(devices) if self.within else []
        self.gathers = devices if self.within else 1
        self.factor_lanes = 3 * self.lanes + self.hidden_lanes
        self.blocks = self.groups * self.gathers
        self.side_rows = -(-self.blocks // 2) * PAIR
        self.block = -(-(model_width + 1) // TILE) * TILE
        self.sum_rows = 256
        self.spare = self.lanes - model_width
        self.sum_parts = -(-model_width // self.spare)
        self.sum_part = self.sum_rows // self.sum_parts
        self.extra_at = self.block - self.sum_rows
        assert self.extra_at % TILE == 0 and self.extra_at + 6 <= self.sum_part
        assert self.sum_rows % (PAIR * self.gathers) == 0
        assert 3 * self.lanes <= self.hidden_lanes

    def shift(self, part):
        return (self.width - part * self.spare) % self.lanes


def scattered(total, radices):
    return [total // math.prod(radices[:k]) for k in range(len(radices))]


def flattened(radices):
    return radices[:1] + ([math.prod(radices[1:])] if len(radices) > 1 else [])


class Peers:
    def __init__(self, radices):
        self.radices = radices
        self.last = len(radices) - 1
        self.strides = [math.prod(radices[:k]) for k in range(len(radices))]
        self.at = lax.axis_index("dp")
        self.digits = [
            (self.at // stride) % radix for stride, radix in zip(self.strides, radices)
        ]

    def other(self, stage, distance):
        digit = (self.digits[stage] + distance) % self.radices[stage]
        return digit, {"dp": self.at + (digit - self.digits[stage]) * self.strides[stage]}

    def everyone(self):
        return [
            self.other(stage, distance)[1]
            for stage in range(len(self.radices))
            for distance in range(1, self.radices[stage])
        ]

    def copies(self, stage, source, target, sends, receives):
        found = []
        for distance in range(1, self.radices[stage]):
            digit, device = self.other(stage, distance)
            found.append(
                pltpu.make_async_remote_copy(
                    src_ref=source(digit),
                    dst_ref=target(distance),
                    send_sem=sends.at[stage, distance - 1],
                    recv_sem=receives.at[stage, distance - 1],
                    device_id=device,
                    device_id_type=MESH_ID,
                )
            )
        return found

    def first(self, stage):
        return sum(
            self.digits[k] * math.prod(self.radices[k + 1 :]) for k in range(stage + 1)
        )


class Gather:
    def __init__(self, peers, blocks, group, sems):
        self.peers, self.blocks, self.group = peers, blocks, group
        self.sends, self.receives = sems.at[0, group], sems.at[1, group]
        self.count = math.prod(peers.radices)

    def copies(self, stage):
        size = math.prod(self.peers.radices[stage + 1 :])
        place = self.blocks.at[pl.ds(self.group * self.count + self.peers.first(stage), size)]
        return self.peers.copies(
            stage, lambda digit: place, lambda distance: place, self.sends, self.receives
        )

    def push(self, stage):
        if stage < self.peers.last:
            self.finish(stage + 1)
        for copy in self.copies(stage):
            copy.start()

    def finish(self, stage):
        for copy in self.copies(stage):
            copy.wait_recv()

    def drain(self):
        for stage in range(self.peers.last + 1):
            for copy in self.copies(stage):
                copy.wait_send()


class Reduction:
    def __init__(self, peers, total, total_low, outgoing, incoming, sems):
        self.peers, self.total, self.total_low = peers, total, total_low
        self.outgoing, self.incoming = outgoing, incoming
        self.scatter_sems, self.share_sems = sems[:2], sems[2:]
        self.stages = peers.last + 1
        self.steps = 2 * self.stages + 1

    def region(self, stage):
        start, length = 0, self.total.shape[0]
        for k in range(stage):
            length //= self.peers.radices[k]
            start = start + self.peers.digits[k] * length
        return start, length

    def scatter_copies(self, stage):
        part = self.region(stage)[1] // self.peers.radices[stage]
        return self.peers.copies(
            stage,
            lambda digit: self.outgoing[stage].at[pl.ds(aligned(digit * part), part)],
            lambda distance: self.incoming[stage].at[distance - 1],
            *self.scatter_sems,
        )

    def share_copies(self, stage):
        start, length = self.region(stage + 1)
        place = self.total_low.at[pl.ds(aligned(start), length)]
        return self.peers.copies(
            stage, lambda digit: place, lambda distance: place, *self.share_sems
        )

    def step(self, at):
        if 1 <= at <= self.stages:
            start, length = self.region(at)
            place = pl.ds(aligned(start), length)
            for index, copy in enumerate(self.scatter_copies(at - 1)):
                copy.wait_recv()
                self.total[place, :] += wide(self.incoming[at - 1][index])
        if at < self.stages:
            start, length = self.region(at)
            self.outgoing[at][...] = low(self.total[pl.ds(aligned(start), length), :])
            for copy in self.scatter_copies(at):
                copy.start()
            return
        if at == self.stages:
            start, length = self.region(at)
            place = pl.ds(aligned(start), length)
            self.total_low[place, :] = low(self.total[place, :])
        else:
            for copy in self.share_copies(2 * self.stages - at):
                copy.wait_recv()
        stage = 2 * self.stages - 1 - at
        if stage >= 0:
            for copy in self.share_copies(stage):
                copy.start()

    def drain(self):
        for stage in range(self.stages):
            for copy in self.scatter_copies(stage) + self.share_copies(stage):
                copy.wait_send()


class LateReduction:
    def __init__(self, near, total, total_low, handed, got, outgoing, incoming, sems):
        self.near, self.total, self.total_low = near, total, total_low
        self.handed, self.got, self.outgoing, self.incoming = handed, got, outgoing, incoming
        self.hand_sems, self.back_sems, self.scatter_sems, self.share_sems = (
            sems[:2], sems[2:4], sems[4:6], sems[6:]
        )
        self.odd = near.digits[0] == 1
        self.chips = near.radices[1] if near.last > 0 else 1
        self.part = total.shape[0] // self.chips

    def hand(self):
        return self.near.copies(
            0, lambda digit: self.handed, lambda distance: self.got, *self.hand_sems
        )[0]

    def back(self):
        return self.near.copies(
            0, lambda digit: self.total_low, lambda distance: self.total_low, *self.back_sems
        )[0]

    def place(self, digit):
        return pl.ds(aligned(digit * self.part), self.part)

    def scatter(self):
        if self.chips == 1:
            return []
        return self.near.copies(
            1,
            lambda digit: self.outgoing.at[self.place(digit)],
            lambda distance: self.incoming.at[distance - 1],
            *self.scatter_sems,
        )

    def share(self):
        if self.chips == 1:
            return []
        own = self.total_low.at[self.place(self.near.digits[1])]
        return self.near.copies(
            1, lambda digit: own, lambda distance: own, *self.share_sems
        )

    def step(self, at):
        if at == 0:

            @pl.when(jnp.logical_not(self.odd))
            def _():
                self.handed[...] = low(self.total[...])
                self.hand().start()

            @pl.when(self.odd)
            def _():
                self.hand().wait_recv()
                self.total[...] += wide(self.got[...])
                self.outgoing[...] = low(self.total[...])
                for copy in self.scatter():
                    copy.start()

        elif at == 1:

            @pl.when(self.odd)
            def _():
                own = self.place(self.near.digits[1] if self.chips > 1 else 0)
                chunk = self.total[own, :]
                for index, copy in enumerate(self.scatter()):
                    copy.wait_recv()
                    chunk = chunk + wide(self.incoming[index])
                self.total_low[own, :] = low(chunk)
                for copy in self.share():
                    copy.start()

        elif at == 2:

            @pl.when(self.odd)
            def _():
                for copy in self.share():
                    copy.wait_recv()
                self.back().start()

        elif at == 3:
            pl.when(jnp.logical_not(self.odd))(lambda: self.back().wait_recv())

    steps = 4

    def drain(self):
        @pl.when(jnp.logical_not(self.odd))
        def _():
            self.hand().wait_send()

        @pl.when(self.odd)
        def _():
            self.back().wait_send()
            for copy in self.scatter() + self.share():
                copy.wait_send()


def layer_kernel(
    z,
    center_ref,
    edge_far,
    counts_ref,
    mask_ref,
    square_far,
    out_far,
    up_far,
    down_far,
    gain_ref,
    bias_ref,
    hidden_ref,
    center_result,
    final_result,
    left_side,
    right_side,
    key_low,
    value_low,
    edge_low,
    norm_result,
    final,
    left_keep,
    right_keep,
    layer_in,
    cotangent,
    got_main,
    got_tail,
    sent_main,
    sent_tail,
    got_center,
    sent_center,
    layer_center,
    normed,
    gated,
    live_grad,
    gate_grad,
    mean_keep,
    scale_keep,
    live_rows,
    live_lanes,
    allowed,
    prob_keep,
    prob_low,
    wide_a,
    wide_b,
    wide_c,
    staging,
    square_rows,
    score_low,
    w_query,
    w_key,
    w_value,
    w_edge,
    w_out,
    w_up,
    w_down,
    rows_keep,
    query_keep,
    key_keep,
    context_keep,
    value_keep,
    score_keep,
    center_low,
    center_wide,
    center_scale,
    hidden_low,
    hidden_wide,
    middle_keep,
    feed_keep,
    row_sums,
    edge_weight_sum,
    left_blocks,
    right_blocks,
    key_sum,
    value_sum,
    edge_sum,
    key_pass,
    value_pass,
    edge_pass,
    send_sem,
    recv_sem,
    center_sem,
    left_sems,
    right_sems,
    key_sems,
    value_sems,
    edge_sems,
    side_sem,
    final_sem,
    turn_sem,
    edge_ref,
    square_ref,
    out_ref,
    up_ref,
    down_ref,
    load_sem,
):
    lanes, width, groups, rows, piece = z.lanes, z.width, z.groups, z.rows, z.piece
    head_size = width // HEADS
    scaling = head_size**-0.5
    inverse = 1.0 / width
    me = lax.axis_index("section")
    partner = {"section": 1 - me}
    peers = Peers(z.radices)
    near = Peers(flattened(z.radices))
    last = peers.last
    turns = z.within and z.radices[:1] == [2] and groups == 3
    core = peers.digits[0] if turns else 0

    share = z.slots // LOADS
    edge_loads = [
        pltpu.make_async_copy(
            edge_far.at[pl.ds(k * share, share)],
            edge_ref.at[pl.ds(k * share, share)],
            load_sem.at[k],
        )
        for k in range(LOADS)
    ]
    weight_loads = [
        pltpu.make_async_copy(source, target, load_sem.at[LOADS + k])
        for k, (source, target) in enumerate(
            (
                (square_far, square_ref),
                (out_far, out_ref),
                (up_far, up_ref),
                (down_far, down_ref),
            )
        )
    ]
    for load in edge_loads + weight_loads:
        load.start()

    barrier = pltpu.get_barrier_semaphore()
    neighbours = [partner] + near.everyone()
    for neighbour in neighbours:
        pl.semaphore_signal(barrier, inc=1, device_id=neighbour, device_id_type=MESH_ID)

    lane = lax.broadcasted_iota(jnp.int32, (1, lanes), 1)
    inside = (lane < width).astype(F32)
    one_lane = (lane == width).astype(F32)
    head_row = lax.broadcasted_iota(jnp.int32, (HEAD_ROWS, lanes), 0)
    head_lane = lax.broadcasted_iota(jnp.int32, (HEAD_ROWS, lanes), 1)
    head_mask = (
        (head_lane >= head_row * head_size)
        & (head_lane < head_row * head_size + head_size)
        & (head_row < HEADS)
    ).astype(F32)
    star_lane = lax.broadcasted_iota(jnp.int32, (TILE, 128), 1)
    star_row = lax.broadcasted_iota(jnp.int32, (TILE, 128), 0)
    own_star = (
        (star_lane >= star_row * HEAD_ROWS) & (star_lane < star_row * HEAD_ROWS + HEAD_ROWS)
    ).astype(F32)
    tail_lane = lax.broadcasted_iota(jnp.int32, (1, 128), 1)

    full = width // PAIR * PAIR

    def prepare(target, first, rest, bias_row):
        count = target.shape[1]
        target[:full, count - 128 :] = jnp.zeros((full, 128), BF16)
        target[:full, : first.shape[1]] = first
        staging[:PAIR, :count] = jnp.zeros((PAIR, count), F32)
        staging[: width - full, : rest.shape[1]] = wide(rest)
        if bias_row is not None:
            staging[width - full : width - full + 1, : bias_row.shape[1]] = wide(bias_row)
        target[full : full + PAIR, :] = low(staging[:PAIR, :count])
        target[full + PAIR :, :] = jnp.zeros((lanes - full - PAIR, count), BF16)

    def prepare_square(target, index, bias_row):
        def strided(start, count):
            return jnp.concatenate(
                [part[pl.ds(start, count, stride=4), :] for part in square_rows], 1
            )[:, :width]

        first = low(strided(index, full))
        rest = strided(index + 4 * full, width - full)
        prepare(target, first, rest, bias_row)

    def take_apart():
        def one(at, carry):
            place = pl.ds(pl.multiple_of(at * TILE, TILE), TILE)
            both = jnp.concatenate([wide(square_ref[2 * at]), wide(square_ref[2 * at + 1])], 0)
            for index, part in enumerate(square_rows):
                piece_lanes = both[:, index * 128 : (index + 1) * 128]
                part[place, : piece_lanes.shape[1]] = piece_lanes
            return carry

        lax.fori_loop(0, width // 2, one, 0, unroll=10)

    def prepare_first():
        weight_loads[0].wait()
        take_apart()
        prepare_square(w_edge, 3, bias_ref[6:7, :])

    def prepare_rest():
        prepare_square(w_query, 0, bias_ref[3:4, :])
        prepare_square(w_key, 1, None)
        prepare_square(w_value, 2, bias_ref[4:5, :])
        for load in weight_loads[1:]:
            load.wait()
        prepare(w_out, out_ref[:full, :], out_ref[full:, :], bias_ref[5:6, :])
        prepare(w_up, up_ref[:full, :], up_ref[full:, :], hidden_ref[...])
        prepare(w_down, down_ref[:full, :], down_ref[full:, :], None)

    rows_keep[...] = jnp.zeros((TILE, lanes), F32)
    rows_keep[0:3, :width] = wide(gain_ref[...])
    rows_keep[3:6, :width] = wide(bias_ref[0:3, :])
    rows_keep[6:7, :width] = wide(bias_ref[7:8, :])
    gain_center = rows_keep[0:1, :]
    gain_edge = rows_keep[1:2, :]
    gain_feed = rows_keep[2:3, :]
    bias_center = rows_keep[3:4, :] + one_lane
    bias_edge = rows_keep[4:5, :] + one_lane
    bias_feed = rows_keep[5:6, :] + one_lane
    bias_down = rows_keep[6:7, :]
    row_sums[...] = jnp.zeros((6, TILE, lanes), F32)
    edge_weight_sum[...] = jnp.zeros((lanes, lanes), F32)

    def unpack_own(target):
        def one(at, carry):
            first = wide(edge_ref[2 * at])
            second = wide(edge_ref[2 * at + 1])
            place = pl.ds(pl.multiple_of(at * PAIR, PAIR), PAIR)
            for group in range(groups):
                part = slice(group * TILE, (group + 1) * TILE)
                target[group, place, :width] = low(
                    jnp.concatenate([first[part], second[part]], 0)
                )
            return carry

        for group in range(groups):
            target[group, :, z.main :] = jnp.zeros((rows, 128), BF16)
        for load in edge_loads:
            load.wait()
        lax.fori_loop(0, z.slots // 2, one, 0, unroll=5)

    def unpack_center(target):
        staging[: z.stars, :lanes] = jnp.zeros((z.stars, lanes), F32)
        staging[: z.stars, :width] = wide(center_ref[...])
        for group in range(groups):
            target[group] = low(pad_rows(staging[group * TILE : (group + 1) * TILE, :lanes]))

    def find_live():
        counts = jnp.zeros((z.stars, z.slots), jnp.int32)
        star_at = lax.broadcasted_iota(jnp.int32, (z.stars, z.slots), 0)
        slot_at = lax.broadcasted_iota(jnp.int32, (z.stars, z.slots), 1)
        for star in range(z.stars):
            counts = jnp.where(star_at == star, counts_ref[star], counts)
        live = ((slot_at < counts) & (mask_ref[...] > 0)).astype(F32)
        spread = low(pad_rows(own_star))
        slots = z.slots // PIECES
        for group in range(groups):
            part = low(pad_rows(live[group * TILE : (group + 1) * TILE]))
            turned = outer_sum(part, spread)
            for at in range(PIECES):
                live_lanes[group, at, :slots, :] = turned[at * slots : (at + 1) * slots]
            allowed[group, rows : rows + TILE, :] = own_star
            allowed[group, rows + TILE :, :] = jnp.zeros((TILE, 128), F32)

    blocks = [(0, z.tall), (z.tall, z.short), (z.tall + z.short, z.short)]

    def spans(at):
        return [pl.ds(pl.multiple_of(at * piece + start, PAIR), count) for start, count in blocks]

    def tail_span(at):
        return pl.ds(pl.multiple_of(at * z.tall, PAIR), z.tall)

    def cut_blocks(values):
        return [values[start : start + count] for start, count in blocks]

    def whole_span(at):
        return pl.ds(pl.multiple_of(at * piece, PAIR), piece)

    def three(column):
        return jnp.concatenate([column] * (lanes // 128), axis=1)

    def open_piece(group, at):
        count = piece // TILE
        slots = live_lanes[group, at][:count]
        here = (jnp.broadcast_to(slots[:, None, :], (count, TILE, 128)) * own_star[None]).reshape(
            piece, 128
        )
        allowed[group, whole_span(at), :] = here
        live_rows[group, whole_span(at), :] = jnp.broadcast_to(
            jnp.max(here, axis=1, keepdims=True), (piece, 128)
        )

    def normalise(values):
        mean = jnp.sum(values, axis=1, keepdims=True) * inverse
        centred = values - mean * inside
        spread = jnp.sum(centred * centred, axis=1, keepdims=True) * inverse
        scale = lax.rsqrt(spread + EPSILON)
        return centred * scale, mean, scale

    def norm_back(unit, scale, grad_unit):
        first = jnp.sum(grad_unit, axis=1, keepdims=True) * inverse
        second = jnp.sum(grad_unit * unit, axis=1, keepdims=True) * inverse
        return scale * (grad_unit - first - unit * second)

    def over_heads(values):
        return jnp.sum(values.reshape(TILE, HEAD_ROWS, lanes) * head_mask[None], axis=1)

    def by_head(values):
        return (values[:, None, :] * head_mask[None]).reshape(TILE * HEAD_ROWS, lanes)

    def piece_copies(group, at):
        main = whole_span(at)
        tail = tail_span(at)
        return [
            pltpu.make_async_remote_copy(
                src_ref=source.at[group, place],
                dst_ref=target.at[group, place],
                send_sem=send_sem.at[group, at, index],
                recv_sem=recv_sem.at[group, at, index],
                device_id=partner,
                device_id_type=MESH_ID,
            )
            for index, (source, target, place) in enumerate(
                ((sent_main, got_main, main), (sent_tail, got_tail, tail))
            )
        ]

    def center_copy(group):
        return pltpu.make_async_remote_copy(
            src_ref=sent_center.at[group],
            dst_ref=got_center.at[group],
            send_sem=center_sem.at[0, group],
            recv_sem=center_sem.at[1, group],
            device_id=partner,
            device_id_type=MESH_ID,
        )

    def only(values, first, count):
        return jnp.where((tail_lane >= first) & (tail_lane < first + count), values, 0.0)

    def put_blocks(group, at, values):
        for place, value in zip(spans(at), values):
            sent_main[group, place, :] = low(value[:, : z.main])
        first, second, third = [only(value[:, z.main :], 0, z.over) for value in values]
        start = 2 * z.over
        below = 0.0
        for k in range(z.short // PAIR):
            shift = start + k * z.spill
            part = pltpu.roll(third[k * PAIR : (k + 1) * PAIR], shift - z.fits, 1)
            below = below + only(part, shift, z.spill)
        beside = pltpu.roll(second, z.over, 1) + only(pltpu.roll(third, start, 1), start, z.fits)
        sent_tail[group, tail_span(at), :] = low(first + jnp.concatenate([beside, below], 0))

    def get_blocks(group, at):
        tail = wide(got_tail[group, tail_span(at), :])
        upper, lower = tail[: z.short], tail[z.short :]
        start = 2 * z.over
        spilt = jnp.concatenate(
            [
                only(pltpu.roll(lower, 128 - start - k * z.spill + z.fits, 1), z.fits, z.spill)
                for k in range(z.short // PAIR)
            ],
            0,
        )
        tails = [
            only(tail, 0, z.over),
            only(pltpu.roll(upper, 128 - z.over, 1), 0, z.over),
            only(pltpu.roll(upper, 128 - start, 1), 0, z.fits) + spilt,
        ]
        return [
            jnp.concatenate([wide(got_main[group, place, :]), part], 1)
            for place, part in zip(spans(at), tails)
        ]

    zero_tile = jnp.zeros((TILE, lanes), F32)

    def fold(values):
        return jnp.sum(values.reshape(values.shape[0] // TILE, TILE, lanes), axis=0)

    def repeated(values):
        return jnp.broadcast_to(
            values[:TILE][None], (z.tall // TILE, TILE, lanes)
        ).reshape(z.tall, lanes)

    def norm_center(group):
        center = wide(layer_center[group])
        unit, _, scale = normalise(center)
        center_norm = low(unit * gain_center + bias_center)
        center_low[0, group] = center_norm
        center_wide[0, group] = unit
        center_scale[0, group] = jnp.broadcast_to(scale, (PAIR, 128))
        normed[group, rows:, :] = low(pad_rows(wide(center_norm)[:TILE]))
        return center_norm

    def ask_center(group):
        query = low(product(center_low[0, group], w_query[...]))
        query_heads = low(by_head(wide(query)[:TILE]))
        query_keep[group] = query_heads
        key_keep[group] = low(against(query_heads, w_key[...]) * scaling)

    def norm_span(group, place, values):
        unit, mean, scale = normalise(values)
        mean_keep[group, place, :] = jnp.broadcast_to(mean, (values.shape[0], 128))
        scale_keep[group, place, :] = jnp.broadcast_to(scale, (values.shape[0], 128))
        edge_norm = low(unit * gain_edge + bias_edge)
        normed[group, place, :] = edge_norm
        return wide(edge_norm)

    def update_span(group, place, changed, values, sums):
        out_sum, update_sum = sums
        update = changed * three(live_rows[group, place, :])
        result = values + update
        return result, (out_sum + fold(result * result), update_sum + fold(update * update))

    def forward_center(group):
        scores = against(normed[group], key_keep[group])
        yield
        open_slots = allowed[group] > 0
        top = jnp.max(jnp.where(open_slots, scores, MASKED_SCORE), axis=0, keepdims=True)
        raised = jnp.where(open_slots, jnp.exp(scores - top), 0.0)
        probs = raised * (1.0 / jnp.sum(raised, axis=0, keepdims=True))
        prob_keep[group] = probs
        probs_low = low(probs)
        prob_low[group] = probs_low
        yield
        context = low(outer_sum(probs_low, normed[group]))
        yield
        context_keep[group] = context
        attended = low(pad_rows(over_heads(product(context, w_value[...]))) + one_lane)
        center_low[1, group] = attended
        yield
        branch_attn = product(attended, w_out[...])
        middle = wide(layer_center[group]) + branch_attn
        yield
        unit, _, scale = normalise(middle)
        center_wide[1, group] = unit
        center_scale[1, group] = jnp.broadcast_to(scale, (PAIR, 128))
        feed_norm = low(unit * gain_feed + bias_feed)
        center_low[2, group] = feed_norm
        hidden = product(feed_norm, w_up[...])
        hidden_wide[group] = hidden
        yield
        feed_keep[group] = middle

    def feed_center(group, target):
        middle = feed_keep[group]
        active = low(gelu_parts(hidden_wide[group])[0])
        hidden_low[0, group] = active
        branch_feed = against(active, w_down[...]) + bias_down
        yield
        center_out = middle + branch_feed
        target[group] = low(pad_rows(center_out[:TILE]))
        branch_attn = middle - wide(layer_center[group])
        for index, measure in ((0, center_out), (2, branch_attn), (4, branch_feed)):
            put_norm(group, index, (measure * measure)[:TILE], width)

    def put_norm(group, index, squares, count):
        measure = jnp.sqrt(jnp.sum(squares, axis=1, keepdims=True) * (1.0 / count))
        norm_result[group] = jnp.where(star_lane == index, measure, norm_result[group])

    def put_edge_norms(group, sums):
        out_sum, update_sum = sums
        put_norm(group, 1, out_sum, width * z.slots)
        put_norm(group, 3, update_sum, width * z.slots)

    def backward_center(group, grad_low):
        grad_center = wide(grad_low)
        center_low[3, group] = grad_low
        grad_active = product(grad_low, w_down[...])
        grad_hidden = low(gelu_parts(hidden_wide[group])[1] * grad_active)
        hidden_low[1, group] = grad_hidden
        yield
        grad_norm = against(grad_hidden, w_up[...])
        unit = center_wide[1, group]
        row_sums[2] += sum_pairs(grad_norm * unit)
        row_sums[5] += sum_pairs(grad_norm)
        grad_middle = grad_center + norm_back(
            unit, center_scale[1, group][:, :1], grad_norm * gain_feed
        )
        middle_keep[group] = grad_middle
        yield
        grad_attn = low(grad_middle)
        center_low[4, group] = grad_attn
        grad_attended = wide(low(against(grad_attn, w_out[...])))
        value_heads = low(by_head(grad_attended[:TILE]))
        value_keep[group] = value_heads
        yield
        value_map = low(against(value_heads, w_value[...]))
        yield
        probs = prob_keep[group]
        weighted = probs * against(normed[group], value_map)
        grad_scores = low(weighted - probs * jnp.sum(weighted, axis=0, keepdims=True))
        wide_b[...] = product(
            jnp.concatenate([prob_low[group], grad_scores], 1),
            jnp.concatenate([value_map, key_keep[group]], 0),
        )
        score_low[...] = grad_scores

    def score_center(group):
        score_sum = low(outer_sum(score_low[...], normed[group]))
        score_keep[group] = score_sum
        yield
        grad_query = low(pad_rows(over_heads(product(score_sum, w_key[...]))) * scaling)
        center_low[5, group] = grad_query
        yield

    def finish_center(group, center_sum, target):
        yield
        grad_norm = (
            against(center_low[5, group], w_query[...])
            + wide_b[rows:, :]
            + pad_rows(center_sum)
        )
        unit = center_wide[0, group]
        row_sums[0] += sum_pairs(grad_norm * unit)
        row_sums[3] += sum_pairs(grad_norm)
        yield
        result = middle_keep[group] + norm_back(
            unit, center_scale[0, group][:, :1], grad_norm * gain_center
        )
        target[group] = low(pad_rows(result[:TILE]))

    def edge_back(group, place, grad_gate, grad_edge, center_pair, sums):
        gain_sum, bias_sum = sums
        grad_norm = wide_b[place, :] + grad_gate * center_pair[: grad_gate.shape[0]]
        scale = three(scale_keep[group, place, :])
        unit = (
            wide(layer_in[group, place, :]) - three(mean_keep[group, place, :]) * inside
        ) * scale
        sums = (gain_sum + fold(grad_norm * unit), bias_sum + fold(grad_norm))
        return grad_edge + norm_back(unit, scale, grad_norm * gain_edge), sums

    def put_block(blocks, group, hidden, parts):
        rest = jnp.zeros((TILE, z.hidden_lanes - 3 * lanes), F32)
        below = [wide(center_low[k, group])[:TILE] for k in parts] + [rest]
        mine = group * z.gathers + (peers.first(last) if z.within else 0)
        blocks[mine] = low(
            jnp.concatenate([wide(hidden_low[hidden, group])[:TILE], jnp.concatenate(below, 1)], 0)
        )

    def left_gather(group):
        return Gather(peers, left_blocks, group, left_sems)

    def right_gather(group):
        return Gather(peers, right_blocks, group, right_sems)

    def push(gather, at):
        if not z.within:
            return
        for behind in range(last + 1):

            @pl.when(at >= behind)
            def _(behind=behind):
                gather(at - behind).push(last - behind)

    def push_rest(gather, behind):
        if not z.within:
            return
        for group in range(groups):
            stage = last - behind - (groups - 1 - group)
            if stage >= 0:
                gather(group).push(stage)

    def push_left(group):
        put_block(left_blocks, group, 0, (0, 1, 2))
        push(left_gather, group)

    def push_right(group):
        put_block(right_blocks, group, 1, (5, 4, 3))
        push(right_gather, group)

    def pack(target, matrix, extra=None):
        target[...] = jnp.where(lane < width, matrix[: z.sum_rows], 0.0)
        staging[: z.sum_part, :lanes] = matrix[z.sum_rows : z.sum_rows + z.sum_part]
        if extra is not None:
            staging[z.extra_at : z.extra_at + 6, :lanes] = extra
        rest = jnp.where(lane < width, staging[: z.sum_part, :lanes], 0.0)
        for part in range(z.sum_parts):
            place = slice(part * z.sum_part, (part + 1) * z.sum_part)
            target[place, :] += jnp.where(lane >= width, pltpu.roll(rest, z.shift(part), 1), 0.0)

    def fill_value():
        pack(value_sum, outer_sum(flat(context_keep[...]), flat(value_keep[...])))

    def fill_key():
        pack(key_sum, outer_sum(flat(score_keep[...]), flat(query_keep[...])) * scaling)

    def fill_edge():
        pack(edge_sum, edge_weight_sum[...], jnp.sum(row_sums[...], axis=1))

    if z.within:
        reductions = {
            "key": Reduction(near, key_sum, key_low, *key_pass, key_sems),
            "value": Reduction(near, value_sum, value_low, *value_pass, value_sems),
            "edge": LateReduction(near, edge_sum, edge_low, *edge_pass, edge_sems),
        }

    def advance(name, number):
        if z.within and number < reductions[name].steps:
            reductions[name].step(number)

    def side_copies(group):
        count = z.gathers * TILE
        place = pl.ds(group * count, count)
        return [
            pltpu.make_async_copy(kept.at[place], side.at[place], side_sem.at[index, group])
            for index, (kept, side) in enumerate(
                ((left_keep, left_side), (right_keep, right_side))
            )
        ]

    def final_copy(group):
        return pltpu.make_async_copy(final.at[group], final_result.at[group], final_sem.at[group])

    def sort_pair(at, first_left, second_left, first_right, second_right):
        place = pl.ds(pl.multiple_of(at * TILE, PAIR), PAIR)
        for first, second, kept in (
            (first_left, second_left, left_keep),
            (first_right, second_right, right_keep),
        ):
            first, second = wide(first), wide(second)
            kept[place, : z.hidden_lanes] = low(jnp.concatenate([first[:TILE], second[:TILE]], 0))
            kept[place, z.hidden_lanes :] = low(
                jnp.concatenate([first[TILE:], second[TILE:]], 0)
            )[:, : 3 * lanes]

    def sort_sides(group):
        left_gather(group).finish(0)
        right_gather(group).finish(0)
        first_block = group * z.gathers

        def one(at, carry):
            at = first_block + 2 * at
            sort_pair(at, *[side[at + k] for side in (left_blocks, right_blocks) for k in (0, 1)])
            return carry

        lax.fori_loop(0, z.gathers // 2, one, 0)
        for copy in side_copies(group):
            copy.start()

    def run(*steps, between=()):
        between = list(between)
        for step in steps:
            for _ in step:
                if between:
                    between.pop(0)()
        for work in between:
            work()

    def send(group, at):
        for copy in piece_copies(group, at):
            copy.start()

    def receive(group, at):
        for copy in piece_copies(group, at):
            copy.wait_recv()

    def gate_span(group, place, edge_norm, center_pair):
        gated[group, place, :] = low(edge_norm * center_pair[: edge_norm.shape[0]])

    def update_piece(group, at, sums):
        wide_a[:piece, :] = product(gated[group, whole_span(at), :], w_edge[...])
        results = []
        for place, changed in zip(spans(at), cut_blocks(wide_a[:piece, :])):
            result, sums = update_span(
                group, place, changed, wide(layer_in[group, place, :]), sums
            )
            results.append(result)
        return results, sums

    def weigh(group, at):
        edge_weight_sum[...] += outer_sum(
            gated[group, whole_span(at), :], live_grad[group, whole_span(at), :]
        )

    @pl.when(me == 0)
    def first_layer():
        unpack_center(layer_center)
        find_live()
        prepare_first()
        unpack_own(layer_in)
        norm_result[...] = jnp.zeros(norm_result.shape, F32)
        pl.semaphore_wait(barrier, len(neighbours))

        def forward_edges(group):
            center_pair = repeated(wide(norm_center(group)))

            def one(at, sums):
                open_piece(group, at)
                for place in spans(at):
                    edge_norm = norm_span(group, place, wide(layer_in[group, place, :]))
                    gate_span(group, place, edge_norm, center_pair)
                results, sums = update_piece(group, at, sums)
                put_blocks(group, at, results)
                at_once = (at < PIECES - 1) & ((group == 0) & (core == 0) if turns else True)
                pl.when(at_once)(lambda: send(group, at))
                return sums

            put_edge_norms(group, lax.fori_loop(0, PIECES, one, (zero_tile, zero_tile)))

        def forward_rest(group):
            @pl.when(group == 0)
            def _():
                prepare_rest()
                if turns:
                    pl.when(core == 0)(lambda: pass_turn(0))

            ask_center(group)
            run(forward_center(group), feed_center(group, sent_center))
            push_left(group)

        def send_rest(group):
            center_copy(group).start()
            send(group, PIECES - 1)

        def take_turn(group):
            pl.semaphore_wait(turn_sem, 1)
            for at in range(PIECES - 1):
                send(group, at)

        def pass_turn(group):
            for at in range(FIRST_PIECES):
                for copy in piece_copies(group, at):
                    copy.wait_send()
            pl.semaphore_signal(
                turn_sem, inc=1, device_id=peers.other(0, 1)[1], device_id_type=MESH_ID
            )

        def forward(step, carry):
            group = step // 2
            pl.when(step % 2 == 0)(lambda: forward_edges(group))
            pl.when(step % 2 == 1)(lambda: forward_rest(group))

            def hook(at, which, *works):
                @pl.when((step == at) & (core == which))
                def _():
                    for work, group in works:
                        work(group)

            if turns:
                hook(1, 0, (send_rest, 0))
                hook(1, 1, (take_turn, 0), (send_rest, 0))
                hook(2, 0, (take_turn, 1))
                hook(2, 1, (pass_turn, 0))
                hook(3, 0, (send_rest, 1), (pass_turn, 1))
                hook(4, 1, (take_turn, 1), (send_rest, 1))
                hook(5, 0, (take_turn, 2), (send_rest, 2))
                hook(5, 1, (pass_turn, 1))
            else:
                pl.when(step % 2 == 1)(lambda: send_rest(group))
            return carry

        lax.fori_loop(0, 2 * groups, forward, 0)
        push_rest(left_gather, 1)

        def backward(group, carry):
            center_copy(group).wait_recv()
            run(backward_center(group, got_center[group]))
            is_last = group == groups - 1

            @pl.when(is_last)
            def _():
                fill_value()
                advance("value", 0)

            run(score_center(group))
            push_right(group)
            if turns:
                pl.when((group == 0) & (core == 0))(lambda: pass_turn(2))

                @pl.when((group == 0) & (core == 1))
                def _():
                    take_turn(2)
                    send_rest(2)


            @pl.when(is_last)
            def _():
                fill_key()
                advance("key", 0)

            @pl.when(group == 0)
            def _():
                for behind in range(2, last + 1):
                    push_rest(left_gather, behind)

            center_pair = repeated(wide(center_low[0, group]))

            def one(at, carry):
                center_sum, sums = carry
                for number in range(PIECES):

                    @pl.when(is_last & (at == number))
                    def _(number=number):
                        if number == 2:
                            if last > 0:
                                push_rest(right_gather, 1)
                        else:
                            names = ("value", "key", "", "value", "key")
                            advance(names[number], number // 3 + 1)

                receive(group, at)
                for place, grad, (start, count) in zip(spans(at), get_blocks(group, at), blocks):
                    wide_c[start : start + count, :] = grad
                    live_grad[group, place, :] = low(grad * three(live_rows[group, place, :]))
                wide_a[:piece, :] = against(live_grad[group, whole_span(at), :], w_edge[...])
                for place, grad_gate, grad in zip(
                    spans(at), cut_blocks(wide_a[:piece, :]), cut_blocks(wide_c[:piece, :])
                ):
                    grad_gate = wide(low(grad_gate))
                    center_sum = center_sum + fold(grad_gate * wide(normed[group, place, :]))
                    result, sums = edge_back(group, place, grad_gate, grad, center_pair, sums)
                    final[group, place, :] = low(result)
                weigh(group, at)
                return center_sum, sums

            center_sum, sums = lax.fori_loop(
                0, PIECES, one, (zero_tile, (zero_tile, zero_tile))
            )
            gain_sum, bias_sum = sums
            row_sums[1] += gain_sum
            row_sums[4] += bias_sum
            run(finish_center(group, center_sum, center_result))
            final_copy(group).start()
            return carry

        lax.fori_loop(0, groups, backward, 0)

    @pl.when(me == 1)
    def second_layer():
        unpack_center(sent_center)
        find_live()
        norm_result[...] = jnp.zeros(norm_result.shape, F32)
        prepare_first()
        unpack_own(cotangent)
        prepare_rest()
        pl.semaphore_wait(barrier, len(neighbours))

        def gate(at, carry):
            group = at // PIECES
            at = at % PIECES
            open_piece(group, at)
            for place in spans(at):
                live_grad[group, place, :] = low(
                    wide(cotangent[group, place, :]) * three(live_rows[group, place, :])
                )
            gate_grad[group, whole_span(at), :] = low(
                against(live_grad[group, whole_span(at), :], w_edge[...])
            )
            return carry

        lax.fori_loop(0, groups * PIECES, gate, 0)

        def get_center(group):
            center_copy(group).wait_recv()
            layer_center[group] = got_center[group]
            norm_center(group)
            ask_center(group)

        def both(group, carry):
            def arrive(at, center_sum):
                pl.when(at == PIECES - 1)(lambda: get_center(group))
                receive(group, at)
                for place, values in zip(spans(at), get_blocks(group, at)):
                    layer_in[group, place, :] = low(values)
                    edge_norm = norm_span(group, place, values)
                    center_sum = center_sum + fold(edge_norm * wide(gate_grad[group, place, :]))
                return center_sum

            center_sum = lax.fori_loop(0, PIECES, arrive, zero_tile)
            center_pair = repeated(wide(center_low[0, group]))
            def leave(at, sums):
                results = []
                for place in spans(at):
                    result, sums = edge_back(
                        group,
                        place,
                        wide(gate_grad[group, place, :]),
                        wide(cotangent[group, place, :]),
                        center_pair,
                        sums,
                    )
                    results.append(result)
                put_blocks(group, at, results)
                send(group, at)
                return sums

            run(forward_center(group), backward_center(group, sent_center[group]))
            run(score_center(group), finish_center(group, center_sum, sent_center))
            center_copy(group).start()
            gain_sum, bias_sum = lax.fori_loop(0, PIECES, leave, (zero_tile, zero_tile))
            row_sums[1] += gain_sum
            row_sums[4] += bias_sum
            run(feed_center(group, center_result))
            push_left(group)
            push_right(group)
            return carry

        def update(group, carry):
            center_pair = repeated(wide(center_low[0, group]))

            def one(at, sums):
                for place in spans(at):
                    gate_span(group, place, wide(normed[group, place, :]), center_pair)
                results, sums = update_piece(group, at, sums)
                for place, result in zip(spans(at), results):
                    final[group, place, :] = low(result)
                weigh(group, at)
                return sums

            put_edge_norms(group, lax.fori_loop(0, PIECES, one, (zero_tile, zero_tile)))
            final_copy(group).start()
            return carry

        lax.fori_loop(0, groups, both, 0)
        fill_value()
        advance("value", 0)
        fill_key()
        advance("key", 0)
        lax.fori_loop(0, groups, update, 0)

    fill_edge()
    if z.within:
        advance("edge", 0)

        @pl.when(me == 1)
        def _():
            advance("value", 1)
            advance("key", 1)
            if last > 0:
                push_rest(left_gather, 1)
                push_rest(right_gather, 1)
            advance("value", 2)
            advance("key", 2)

        advance("edge", 1)
        advance("value", 3)
        advance("key", 3)
        for behind in range(2, last + 1):
            pl.when(me == 1)(lambda behind=behind: push_rest(left_gather, behind))
            push_rest(right_gather, behind)
        sort_sides(0)
        advance("edge", 2)
        advance("value", 4)
        advance("key", 4)
        for pair in range(1, groups):
            sort_sides(pair)
        advance("edge", 3)
        for reduction in reductions.values():
            reduction.drain()
        for group in range(groups):
            left_gather(group).drain()
            right_gather(group).drain()
            for copy in side_copies(group):
                copy.wait()
    else:
        fill_value()
        fill_key()
        for total, total_low in (
            (key_sum, key_low), (value_sum, value_low), (edge_sum, edge_low)
        ):
            total_low[...] = low(total[...])
        for at in range(0, z.blocks, 2):
            after = min(at + 1, z.blocks - 1)
            keep = 1.0 if at + 1 < z.blocks else 0.0
            sort_pair(
                at,
                left_blocks[at],
                wide(left_blocks[after]) * keep,
                right_blocks[at],
                wide(right_blocks[after]) * keep,
            )
        pltpu.sync_copy(left_keep, left_side)
        pltpu.sync_copy(right_keep, right_side)
    for group in range(groups):
        final_copy(group).wait()

    def sent(group, carry):
        center_copy(group).wait_send()
        for at in range(PIECES):
            waits = [copy.wait_send for copy in piece_copies(group, at)]
            if turns and at < FIRST_PIECES:
                pl.when((me == 1) | ((group == groups - 1) & (core == 1)))(
                    lambda waits=waits: [wait() for wait in waits] and None
                )
            else:
                for wait in waits:
                    wait()
        return carry

    lax.fori_loop(0, groups, sent, 0)


def result_kernel(
    z,
    center_ref,
    final,
    left_side,
    right_side,
    key_low,
    value_low,
    edge_low,
    norm_ref,
    center_result,
    edge_result,
    grad_square,
    grad_out,
    grad_up,
    grad_down,
    grad_gains,
    grad_biases,
    grad_hidden,
    norm_result,
):
    lanes, width, hidden, block = z.lanes, z.width, z.hidden, z.block
    lead = z.hidden_lanes

    def assemble(at, carry):
        place = pl.ds(pl.multiple_of(at * PAIR, PAIR), PAIR)
        parts = [wide(final[group, place, :]) for group in range(z.groups)]
        edge_result[2 * at] = low(jnp.concatenate([part[:TILE] for part in parts], 0))[:, :width]
        edge_result[2 * at + 1] = low(jnp.concatenate([part[TILE:] for part in parts], 0))[
            :, :width
        ]
        return carry

    lax.fori_loop(0, z.slots // 2, assemble, 0, unroll=2)
    center_result[...] = low(
        jnp.concatenate([wide(center_ref[group])[:TILE] for group in range(z.groups)], 0)
    )[:, :width]
    def part(side, index):
        return side[:, lead + index * lanes : lead + (index + 1) * lanes]

    query = outer_sum(part(left_side, 0), part(right_side, 0))
    attend = outer_sum(part(left_side, 1), part(right_side, 1))
    grow = outer_sum(part(left_side, 2), right_side[:, :lead])
    shrink = outer_sum(part(right_side, 2), left_side[:, :lead])
    lane = lax.broadcasted_iota(jnp.int32, (1, lanes), 1)

    def unpack(packed):
        rest = jnp.zeros((z.sum_part, lanes), F32)
        for index in range(z.sum_parts):
            held = wide(packed[index * z.sum_part : (index + 1) * z.sum_part, :])
            held = jnp.where(lane >= width, held, 0.0)
            rest = rest + pltpu.roll(held, (lanes - z.shift(index)) % lanes, 1)
        return jnp.concatenate([wide(packed[...]), rest], 0)

    key, value, edge = unpack(key_low), unpack(value_low), unpack(edge_low)
    sums = edge[block:]
    grad_square[:, 0, :] = query[:width, :width]
    grad_square[:, 1, :] = key[:width, :width]
    grad_square[:, 2, :] = value[:width, :width]
    grad_square[:, 3, :] = edge[:width, :width]
    grad_out[:, 0, :] = attend[:width, :width]
    grad_up[:, 0, :] = grow[:width, :hidden]
    grad_down[:, 0, :] = shrink[:width, :hidden]
    grad_gains[:, 0, :] = sums[0:3, :width]
    grad_biases[0:3, :] = sums[3:6, :width]
    for index, source in ((3, query), (4, value), (5, attend), (6, edge)):
        grad_biases[index : index + 1, :] = source[width : width + 1, :width]
    grad_biases[7:8, :] = jnp.sum(
        wide(part(right_side, 2)), axis=0, keepdims=True
    )[:, :width]
    grad_hidden[...] = grow[width : width + 1, :hidden]
    turned = jnp.concatenate([norm_ref[group] for group in range(z.groups)], 0).T
    norm_result[:, 0, :] = turned[:5]


def on_device(
    center_data,
    edge_data,
    leaf_counts,
    leaf_mask,
    square_weights,
    out_weight,
    up_weight,
    down_weight,
    norm_gains,
    biases,
    hidden_bias,
):
    star_count, model_width = center_data.shape[1:]
    slot_count = edge_data.shape[2]
    hidden_width = up_weight.shape[2]
    z = Sizes(star_count, slot_count, model_width, hidden_width, lax.axis_size("dp"))
    lanes, groups, rows = z.lanes, z.groups, z.rows
    heads = TILE * HEAD_ROWS
    stages = max(len(z.radices), 1)
    most = max(z.radices + [2])
    vmem = pltpu.VMEM
    shape = jax.ShapeDtypeStruct
    dma = pltpu.SemaphoreType.DMA

    def scatter_scratch(total, radices):
        sizes = scattered(total, radices)
        return (
            [vmem((size, lanes), BF16) for size in sizes],
            [vmem((r - 1, size // r, lanes), BF16) for size, r in zip(sizes, radices)],
        )

    near = flattened(z.radices)
    chips = near[1] if len(near) > 1 else 1
    sum_pass = scatter_scratch(z.sum_rows, near)
    sum_sems = [dma((max(len(near), 1), max(near + [2]) - 1))] * 4
    far, close = pl.BlockSpec(memory_space=pltpu.HBM), pl.BlockSpec(memory_space=vmem)
    between = pl.pallas_call(
        functools.partial(layer_kernel, z),
        out_shape=(
            shape((groups, PAIR, lanes), BF16),
            shape((groups, rows, lanes), BF16),
            shape((z.side_rows, z.factor_lanes), BF16),
            shape((z.side_rows, z.factor_lanes), BF16),
            shape((z.sum_rows, lanes), BF16),
            shape((z.sum_rows, lanes), BF16),
            shape((z.sum_rows, lanes), BF16),
            shape((groups, TILE, 128), F32),
        ),
        in_specs=[
            pl.BlockSpec(memory_space=pltpu.SMEM)
            if index == 2
            else far
            if index in (1, 4, 5, 6, 7)
            else close
            for index in range(11)
        ],
        out_specs=[far if index in (1, 2, 3) else close for index in range(8)],
        scratch_shapes=[
            vmem((groups, rows, lanes), BF16),
            vmem((z.side_rows, z.factor_lanes), BF16),
            vmem((z.side_rows, z.factor_lanes), BF16),
            vmem((groups, rows, lanes), BF16),
            vmem((groups, rows, lanes), BF16),
            vmem((groups, rows, z.main), BF16),
            vmem((groups, PIECES * z.tall, 128), BF16),
            vmem((groups, rows, z.main), BF16),
            vmem((groups, PIECES * z.tall, 128), BF16),
            vmem((groups, PAIR, lanes), BF16),
            vmem((groups, PAIR, lanes), BF16),
            vmem((groups, PAIR, lanes), BF16),
            vmem((groups, rows + PAIR, lanes), BF16),
            vmem((groups, rows, lanes), BF16),
            vmem((groups, rows, lanes), BF16),
            vmem((groups, rows, lanes), BF16),
            vmem((groups, rows, 128), F32),
            vmem((groups, rows, 128), F32),
            vmem((groups, rows, 128), F32),
            vmem((groups, PIECES, -(-z.slots // PIECES // TILE) * TILE, 128), F32),
            vmem((groups, rows + PAIR, 128), F32),
            vmem((groups, rows + PAIR, 128), F32),
            vmem((groups, rows + PAIR, 128), BF16),
            vmem((rows, lanes), F32),
            vmem((rows + PAIR, lanes), F32),
            vmem((rows, lanes), F32),
            vmem((max(z.sum_part, z.stars), z.hidden_lanes), F32),
            [vmem((4 * model_width, 128), F32)] * (lanes // 128),
            vmem((rows + PAIR, 128), BF16),
            vmem((lanes, lanes), BF16),
            vmem((lanes, lanes), BF16),
            vmem((lanes, lanes), BF16),
            vmem((lanes, lanes), BF16),
            vmem((lanes, lanes), BF16),
            vmem((lanes, z.hidden_lanes), BF16),
            vmem((lanes, z.hidden_lanes), BF16),
            vmem((TILE, lanes), F32),
            vmem((groups, heads, lanes), BF16),
            vmem((groups, heads, lanes), BF16),
            vmem((groups, heads, lanes), BF16),
            vmem((groups, heads, lanes), BF16),
            vmem((groups, heads, lanes), BF16),
            vmem((6, groups, PAIR, lanes), BF16),
            vmem((2, groups, PAIR, lanes), F32),
            vmem((2, groups, PAIR, 128), F32),
            vmem((2, groups, PAIR, z.hidden_lanes), BF16),
            vmem((groups, PAIR, z.hidden_lanes), F32),
            vmem((groups, PAIR, lanes), F32),
            vmem((groups, PAIR, lanes), F32),
            vmem((6, TILE, lanes), F32),
            vmem((lanes, lanes), F32),
            vmem((z.blocks, PAIR, z.hidden_lanes), BF16),
            vmem((z.blocks, PAIR, z.hidden_lanes), BF16),
            vmem((z.sum_rows, lanes), F32),
            vmem((z.sum_rows, lanes), F32),
            vmem((z.sum_rows, lanes), F32),
            sum_pass,
            sum_pass,
            [
                vmem((z.sum_rows, lanes), BF16),
                vmem((z.sum_rows, lanes), BF16),
                vmem((z.sum_rows, lanes), BF16),
                vmem((max(chips - 1, 1), z.sum_rows // chips, lanes), BF16),
            ],
            dma((groups, PIECES, 2)),
            dma((groups, PIECES, 2)),
            dma((2, groups)),
            dma((2, groups, stages, most - 1)),
            dma((2, groups, stages, most - 1)),
            sum_sems,
            sum_sems,
            sum_sems * 2,
            dma((2, groups)),
            dma((groups,)),
            pltpu.SemaphoreType.REGULAR,
            vmem((slot_count, star_count, model_width), BF16),
            vmem((model_width, 4, model_width), BF16),
            vmem((model_width, model_width), BF16),
            vmem((model_width, hidden_width), BF16),
            vmem((model_width, hidden_width), BF16),
            dma((4 + LOADS,)),
        ],
        compiler_params=pltpu.CompilerParams(
            collective_id=0, has_side_effects=True, vmem_limit_bytes=60 * 1024 * 1024
        ),
    )(
        center_data[0],
        jnp.transpose(edge_data[0], (1, 0, 2)),
        leaf_counts,
        leaf_mask,
        jnp.transpose(square_weights[0], (1, 0, 2)),
        out_weight[0],
        up_weight[0],
        down_weight[0].T,
        norm_gains[0],
        biases[0],
        hidden_bias,
    )
    outputs = pl.pallas_call(
        functools.partial(result_kernel, z),
        out_shape=(
            shape((star_count, model_width), BF16),
            shape((slot_count, star_count, model_width), BF16),
            shape((model_width, 4, model_width), F32),
            shape((model_width, 1, model_width), F32),
            shape((model_width, 1, hidden_width), F32),
            shape((model_width, 1, hidden_width), F32),
            shape((3, 1, model_width), F32),
            shape((8, model_width), F32),
            shape((1, hidden_width), F32),
            shape((5, 1, star_count), F32),
        ),
        in_specs=[pl.BlockSpec(memory_space=vmem)] * 8,
        out_specs=[pl.BlockSpec(memory_space=vmem)] * 10,
        compiler_params=pltpu.CompilerParams(vmem_limit_bytes=60 * 1024 * 1024),
    )(*between)
    center_result, edge_result, *sums, norm_rows = outputs
    if not z.within:
        sums = lax.psum(sums, "dp")
    square_sum, out_sum, up_sum, down_sum, gain_sum, bias_sum, hidden_sum = sums
    return (
        center_result[None],
        jnp.transpose(edge_result, (1, 0, 2))[None],
        jnp.transpose(square_sum, (1, 0, 2))[None],
        jnp.transpose(out_sum, (1, 0, 2)),
        jnp.transpose(up_sum, (1, 0, 2)),
        jnp.transpose(down_sum, (1, 2, 0)),
        jnp.transpose(gain_sum, (1, 0, 2)),
        bias_sum[None],
        hidden_sum,
        jnp.transpose(norm_rows, (1, 0, 2)),
    )


def solution(mesh):
    return jax.shard_map(
        on_device,
        mesh=mesh,
        in_specs=(
            P("section", "dp", None),
            P("section", "dp", None, None),
            P("dp"),
            P("dp", None),
            P("section", None, None, None),
            P("section", None, None),
            P("section", None, None),
            P("section", None, None),
            P("section", None, None),
            P("section", None, None),
            P("section", None),
        ),
        out_specs=(
            P("section", "dp", None),
            P("section", "dp", None, None),
            P("section", None, None, None),
            P("section", None, None),
            P("section", None, None),
            P("section", None, None),
            P("section", None, None),
            P("section", None, None),
            P("section", None),
            P("section", None, "dp"),
        ),
        check_vma=False,
    )
```
